512 devices in a mesh: station: 512 (over z, y, x, core).
Axes of the slice: x: 4, y: 4, z: 16, core: 2. Of those that a mesh axis runs over, the one named last changes fastest.
Arguments:
- right_side: float32 [512, 512, 128], P('station'), may hold values from -6 to 6
- diag_blocks: float32 [512, 512, 512], P('station'), may hold values from -1 to 7
- lower_blocks: float32 [512, 512, 512], P('station'), may hold values from -0.15625 to 0.15625
- upper_blocks: float32 [512, 512, 512], P('station'), may hold values from -0.15625 to 0.15625
- approx_inverse: float32 [512, 512, 512], P('station'), may hold values from -1 to 1
Outputs:
- solution: float32 [512, 512, 128], P('station')
- residual: float32 [512, 512, 128], P('station')
The draws below stay inside these ranges and needn't reach their ends.
All inputs are finite; a program needn't handle non-finite values.
Results may differ from the reference program's by a relative error of at most 0.0003.
Values sent between devices are 32-bit elements; how exact they have to be, the bound alone decides.
No kernel may reach another device: no remote copies, remote signals or barrier semaphores. Data moves between devices by JAX's collectives and lax.ppermute only.
A program may use at most 64 MiB of HBM per device.

```python
import jax
import jax.numpy as jnp
from jax import lax

M = 512
R = 128
ITERS = 2
STATIONS = 512


def off_part(key):
    return jax.random.truncated_normal(key, -4.0, 4.0, (STATIONS, M, M), jnp.float32)


def shared_parts(key):
    key_diag = jax.random.fold_in(key, 11)
    key_off = jax.random.fold_in(key, 12)
    leading = jax.random.uniform(key_diag, (STATIONS, M), jnp.float32, 3.0, 6.0)
    outside = off_part(key_off) * (0.5 / M ** 0.5)
    return (leading, outside)


def draw_diag_blocks(key, part):
    leading, outside = shared_parts(key)
    identity = jnp.eye(M, dtype=jnp.float32)
    return outside + leading[:, :, None] * identity[None, :, :]


def draw_approx_inverse(key, part):
    leading, outside = shared_parts(key)
    key_jitter = jax.random.fold_in(key, 21)
    key_extra = jax.random.fold_in(key, 22)
    recip = 1.0 / leading
    jitter = jax.random.uniform(key_jitter, (STATIONS, M), jnp.float32, 0.9, 1.1)
    identity = jnp.eye(M, dtype=jnp.float32)
    neumann = -(recip[:, :, None] * outside * recip[:, None, :])
    extra = off_part(key_extra) * (0.02 / M ** 0.5)
    return neumann + extra + (recip * jitter)[:, :, None] * identity[None, :, :]


def block_levels(stream_key, shape, shards, least, largest):
    def one(dim, parts):
        steps = jax.random.uniform(jax.random.fold_in(jax.random.fold_in(stream_key, 6), dim), (parts,), jnp.float32, least / len(shards), largest / len(shards))
        return jnp.repeat(jnp.exp(steps), shape[dim] // parts).reshape((-1,) + (1,) * (len(shape) - dim - 1))

    loudness = one(*shards[0])
    for cut in shards[1:]:
        loudness = loudness * one(*cut)
    return loudness


def scatter_about(stream_key, dims, spread, reach, pieces=(), held_as=jnp.bfloat16):
    array = jax.random.normal(stream_key, dims, jnp.float32) * spread
    if len(pieces) > 0:
        array = block_levels(stream_key, dims, pieces, -0.22, 0.18) * array
    return jnp.clip(array, min=-reach, max=reach).astype(held_as)


def setup_inputs(seed: int = 0) -> dict:
    key_list = jax.random.split(jax.random.key(seed), 6)
    right_side = scatter_about(key_list[0], (STATIONS, M, R), 1.0, 6.0, ((0, 512),), jnp.float32)
    diag_blocks = draw_diag_blocks(jax.random.fold_in(key_list[5], 71), 0)
    lower_blocks = scatter_about(key_list[2], (STATIONS, M, M), (3 * M) ** -0.5, 0.15625, ((0, 512),), jnp.float32)
    upper_blocks = scatter_about(key_list[3], (STATIONS, M, M), (3 * M) ** -0.5, 0.15625, ((0, 512),), jnp.float32)
    approx_inverse = draw_approx_inverse(jax.random.fold_in(key_list[5], 71), 0)
    return {"right_side": right_side, "diag_blocks": diag_blocks, "lower_blocks": lower_blocks, "upper_blocks": upper_blocks, "approx_inverse": approx_inverse}


def product(matrix, vector):
    return jnp.einsum("sij,sjk->sik", matrix, vector, precision=lax.Precision.HIGHEST)


def reference(right_side, diag_blocks, lower_blocks, upper_blocks, approx_inverse):
    solution = jnp.zeros_like(right_side)
    residual = right_side
    for iteration in range(ITERS):
        first_pass = product(approx_inverse, residual)
        reduced = residual - product(lower_blocks, jnp.roll(first_pass, 1, axis=0)) - product(upper_blocks, jnp.roll(first_pass, -1, axis=0))
        second_pass = product(approx_inverse, reduced)
        left_part = product(approx_inverse, product(lower_blocks, jnp.roll(second_pass, 1, axis=0)))
        right_part = product(approx_inverse, product(upper_blocks, jnp.roll(second_pass, -1, axis=0)))
        twice_reduced = reduced + product(lower_blocks, jnp.roll(left_part, 1, axis=0)) + product(upper_blocks, jnp.roll(right_part, -1, axis=0))
        solution = solution + product(approx_inverse, twice_reduced)
        residual = right_side - product(lower_blocks, jnp.roll(solution, 1, axis=0)) - product(diag_blocks, solution) - product(upper_blocks, jnp.roll(solution, -1, axis=0))
    return (solution, residual)
```

```python
import jax
import jax.numpy as jnp
from jax import lax
from jax.experimental import pallas as pl
from jax.experimental.pallas import tpu as pltpu
from jax.sharding import PartitionSpec as P

F32 = jnp.float32
BF16 = jnp.bfloat16
VMEM = pl.BlockSpec(memory_space=pltpu.VMEM)
SMEM = pl.BlockSpec(memory_space=pltpu.SMEM)
AXIS = "station"


def split(v):
    high = v.astype(BF16)
    return high, (v - high.astype(F32)).astype(BF16)


def times(matrix, v):
    both = jnp.concatenate(split(v), axis=1)
    out = jnp.dot(matrix[0][...], both, preferred_element_type=F32)
    out += jnp.dot(matrix[1][...], both, preferred_element_type=F32)
    n = v.shape[1]
    return out[:, :n] + out[:, n:]


def put_split(pair, value, at=None):
    high, low = split(value)
    if at is None:
        pair[0][...], pair[1][...] = high, low
    else:
        pair[0][:, at], pair[1][:, at] = high, low


def setup_kernel(odd, rhs, lower, upper, diag, inverse, w, h, e0, e1, n0, n1, f0, f1, d0, d1, j0, j1, h0, h1):
    e, n, f = (e0, e1), (n0, n1), (f0, f1)
    put_split(e, inverse[...])
    w[...] = times(e, rhs[...])
    is_odd = odd[0] == 1
    cols = rhs.shape[1]
    for k in range(inverse.shape[1] // cols):
        at = pl.ds(k * cols, cols)
        low, up = lower[:, at], upper[:, at]
        near = jnp.where(is_odd, low, up)
        far = jnp.where(is_odd, up, low)
        put_split(n, near, at)
        put_split(f, far, at)
        put_split((d0, d1), diag[:, at], at)
        put_split((j0, j1), times(e, near), at)
        product = times(e, far)
        put_split((h0, h1), product, at)
        h[k] = product


def first_pair_kernel(odd, w, near, j0, j1, h, out):
    blocks = h.shape[0]
    out[:blocks] = h[...]
    out[blocks] = w[...]
    out[blocks + 1] = w[...] - times((j0, j1), near[1 - odd[0]])


def pair_kernel(odd, w, near, j0, j1, out):
    out[0] = w[...]
    out[1] = w[...] - times((j0, j1), near[1 - odd[0]])


def second_pass(odd, sent, got, at, h, k, pair, s_far):
    w, ps = sent[at], sent[at + 1]
    w_far, ps_far = got[odd[0], at], got[odd[0], at + 1]
    pair[0] = ps - times(h, w_far)
    sf = ps_far - times(k, w)
    s_far[...] = sf
    pair[1] = times(h, sf)


def first_second_kernel(odd, sent, got, h0, h1, pair, s_far, k0, k1):
    blocks = sent.shape[0] - 2
    cols = sent.shape[2]
    for i in range(blocks):
        put_split((k0, k1), got[odd[0], i], pl.ds(i * cols, cols))
    second_pass(odd, sent, got, blocks, (h0, h1), (k0, k1), pair, s_far)


def second_kernel(odd, sent, got, h0, h1, k0, k1, pair, s_far):
    second_pass(odd, sent, got, 0, (h0, h1), (k0, k1), pair, s_far)


def parts_kernel(odd, near, j0, j1, out):
    n = near.shape[3]
    v = jnp.concatenate([near[1 - odd[0], 0], near[1 - odd[0], 1]], axis=1)
    both = times((j0, j1), v)
    out[0], out[1] = both[:, :n], both[:, n:]


def step_kernel(odd, pair, s_far, sent, got, r, h0, h1, k0, k1, d0, d1, f0, f1, d, rest):
    m, u = sent[0], sent[1]
    m_far, u_far = got[odd[0], 0], got[odd[0], 1]
    step = pair[0] + u + times((h0, h1), m_far)
    step_far = s_far[...] + u_far + times((k0, k1), m)
    d[...] = step
    rest[...] = r[...] - times((d0, d1), step) - times((f0, f1), step_far)


def residual_kernel(odd, near, rest, n0, n1, e0, e1, r, w):
    value = rest[...] - times((n0, n1), near[1 - odd[0]])
    r[...] = value
    w[...] = times((e0, e1), value)


def last_kernel(odd, near, rest, n0, n1, first, d, x, r):
    r[0] = rest[...] - times((n0, n1), near[1 - odd[0]])
    x[0] = first[...] + d[...]


def call(kernel, outs, *args):
    return pl.pallas_call(
        kernel,
        out_shape=[jax.ShapeDtypeStruct(shape, dtype) for shape, dtype in outs],
        in_specs=[SMEM] + [VMEM] * (len(args) - 1),
        out_specs=[VMEM] * len(outs),
        compiler_params=pltpu.CompilerParams(vmem_limit_bytes=24 * 1024 * 1024),
    )(*args)


def local(right_side, diag_blocks, lower_blocks, upper_blocks, approx_inverse):
    count = lax.axis_size(AXIS)
    near_groups = [[i, i + 1] for i in range(0, count, 2)]
    far_groups = [[i + 1, (i + 2) % count] for i in range(0, count, 2)]

    def near(v):
        return lax.all_gather(v, AXIS, axis_index_groups=near_groups)

    def far(v):
        return lax.all_gather(v, AXIS, axis_index_groups=far_groups)

    odd = (lax.axis_index(AXIS) % 2).astype(jnp.int32).reshape(1)
    b = right_side[0]
    size, cols = b.shape
    blocks = size // cols
    vec = ((size, cols), F32)
    two = ((2, size, cols), F32)
    half = [((size, size), BF16)] * 2

    w, h, *mats = call(
        setup_kernel, [vec, ((blocks, size, cols), F32)] + half * 6,
        odd, b, lower_blocks[0], upper_blocks[0], diag_blocks[0], approx_inverse[0],
    )
    E, N, F, D, J, H = (mats[i:i + 2] for i in range(0, 12, 2))
    (sent,) = call(first_pair_kernel, [((blocks + 2, size, cols), F32)], odd, w, near(w), *J, h)
    pair, s_far, *K = call(first_second_kernel, [two, vec] + half, odd, sent, far(sent), *H)
    (parts,) = call(parts_kernel, [two], odd, near(pair), *J)
    d1, rest = call(step_kernel, [vec, vec], odd, pair, s_far, parts, far(parts), b, *H, *K, *D, *F)
    r, w = call(residual_kernel, [vec, vec], odd, near(d1), rest, *N, *E)
    (sent,) = call(pair_kernel, [two], odd, w, near(w), *J)
    pair, s_far = call(second_kernel, [two, vec], odd, sent, far(sent), *H, *K)
    (parts,) = call(parts_kernel, [two], odd, near(pair), *J)
    d2, rest = call(step_kernel, [vec, vec], odd, pair, s_far, parts, far(parts), r, *H, *K, *D, *F)
    one = ((1, size, cols), F32)
    return tuple(call(last_kernel, [one, one], odd, near(d2), rest, *N, d1, d2))


def solution(mesh):
    spec = P(AXIS, None, None)
    return jax.shard_map(local, mesh=mesh, in_specs=(spec,) * 5, out_specs=(spec, spec), check_vma=False)
```

```python
import jax
import jax.numpy as jnp
from jax import lax
from jax.experimental import pallas as pl
from jax.experimental.pallas import tpu as pltpu
from jax.sharding import PartitionSpec as P

F32 = jnp.float32
BF16 = jnp.bfloat16
VMEM = pl.BlockSpec(memory_space=pltpu.VMEM)
SMEM = pl.BlockSpec(memory_space=pltpu.SMEM)
HBM = pl.BlockSpec(memory_space=pltpu.HBM)
ANY = pl.BlockSpec(memory_space=pl.ANY)
AXIS = "station"
ROWS = 128
COST = 8 * 512 * 512 * 128


def split(v):
    high = v.astype(BF16)
    return high, (v - high.astype(F32)).astype(BF16)


def stack(v):
    return jnp.concatenate(split(v), axis=1)


def rows_times(matrix, rows, both):
    out = jnp.dot(matrix[0][rows, :], both, preferred_element_type=F32)
    out += jnp.dot(matrix[1][rows, :], both, preferred_element_type=F32)
    n = both.shape[1] // 2
    return out[:, :n] + out[:, n:]


def blocks_of(size):
    return [pl.ds(k, ROWS) for k in range(0, size, ROWS)]


def times(matrix, v):
    both = stack(v)
    return jnp.concatenate([rows_times(matrix, rows, both) for rows in blocks_of(v.shape[0])], axis=0)


def put_split(pair, value, *at):
    index = at if at else (...,)
    pair[0][index], pair[1][index] = split(value)


def first_kernel(odd, rhs, lower, upper, inverse, w, e0, e1, n0, n1, b_in, e_in, n_in, b_sem, e_sem, n_sem):
    cuts = blocks_of(inverse.shape[0])
    is_odd = odd[0] == 1
    b_copy = pltpu.make_async_copy(rhs, b_in, b_sem)
    b_copy.start()
    e_copies, n_copies = [], []
    for k, rows in enumerate(cuts):
        copy = pltpu.make_async_copy(inverse.at[rows], e_in.at[rows], e_sem.at[k])
        copy.start()
        e_copies.append(copy)
    for k, rows in enumerate(cuts):
        low = pltpu.make_async_copy(lower.at[rows], n_in.at[rows], n_sem.at[k])
        up = pltpu.make_async_copy(upper.at[rows], n_in.at[rows], n_sem.at[k])
        pl.when(is_odd)(low.start)
        pl.when(jnp.logical_not(is_odd))(up.start)
        n_copies.append(low)
    b_copy.wait()
    both = stack(b_in[...])
    for k, rows in enumerate(cuts):
        e_copies[k].wait()
        put_split((e0, e1), e_in[rows], rows)
        w[rows] = rows_times((e0, e1), rows, both)
    for k, rows in enumerate(cuts):
        n_copies[k].wait()
        put_split((n0, n1), n_in[rows], rows)


def first_pair_kernel(odd, w, near, n0, n1, e0, e1, out):
    out[0] = w[...]
    out[1] = w[...] - times((e0, e1), times((n0, n1), near[1 - odd[0]]))


def far_block_kernel(odd, _, lower, upper, e0, e1, h, f0, f1, h0, h1):
    cols = h.shape[2]
    for k in range(h.shape[0]):
        at = pl.ds(k * cols, cols)
        far = jnp.where(odd[0] == 1, upper[:, at], lower[:, at])
        put_split((f0, f1), far, slice(None), at)
        product = times((e0, e1), far)
        h[k] = product
        put_split((h0, h1), product, slice(None), at)


def near_block_kernel(_, diag, e0, e1, n0, n1, d0, d1, j0, j1):
    cols = ROWS
    for k in range(0, diag.shape[1], cols):
        at = pl.ds(k, cols)
        put_split((d0, d1), diag[:, at], slice(None), at)
        both = jnp.concatenate([n0[:, at], n1[:, at]], axis=1)
        for rows in blocks_of(diag.shape[0]):
            put_split((j0, j1), rows_times((e0, e1), rows, both), rows, at)


def second_kernel(sent, got, h0, h1, s):
    s[...] = sent[1] - times((h0, h1), got[0])


def k_kernel(sent, got, k_in, h0, h1, f, s_far, k0, k1):
    cols = k_in.shape[2]
    for i in range(k_in.shape[0]):
        put_split((k0, k1), k_in[i], slice(None), pl.ds(i * cols, cols))
    value = got[1] - times((k0, k1), sent[0])
    s_far[...] = value
    f[...] = times((h0, h1), value)


def part_kernel(odd, near, j0, j1, out):
    out[...] = times((j0, j1), near[1 - odd[0]])


def parts_kernel(odd, m, near, j0, j1, out):
    out[0] = m[...]
    out[1] = times((j0, j1), near[1 - odd[0]])


def pair_kernel(odd, w, near, j0, j1, out):
    out[0] = w[...]
    out[1] = w[...] - times((j0, j1), near[1 - odd[0]])


def seconds_kernel(sent, got, h0, h1, k0, k1, pair, s_far):
    value = got[1] - times((k0, k1), sent[0])
    s_far[...] = value
    pair[0] = sent[1] - times((h0, h1), got[0])
    pair[1] = times((h0, h1), value)


def both_parts_kernel(near, j0, j1, out):
    out[0] = times((j0, j1), near[0])
    out[1] = times((j0, j1), near[1])


def step(s, s_far, sent, got, r, H, K, D, F, d, rest):
    change = s[...] + sent[1] + times(H, got[0])
    far = s_far[...] + got[1] + times(K, sent[0])
    d[...] = change
    rest[...] = r[...] - times(D, change) - times(F, far)


def step_kernel(s, s_far, sent, got, r, h0, h1, k0, k1, d0, d1, f0, f1, d, rest):
    step(s, s_far, sent, got, r, (h0, h1), (k0, k1), (d0, d1), (f0, f1), d, rest)


def pair_step_kernel(pair, s_far, sent, got, r, h0, h1, k0, k1, d0, d1, f0, f1, d, rest):
    step(pair.at[0], s_far, sent, got, r, (h0, h1), (k0, k1), (d0, d1), (f0, f1), d, rest)


def residual_kernel(odd, near, rest, n0, n1, e0, e1, r, w):
    value = rest[...] - times((n0, n1), near[1 - odd[0]])
    r[...] = value
    w[...] = times((e0, e1), value)


def last_kernel(odd, near, rest, n0, n1, first, d, x, r):
    r[0] = rest[...] - times((n0, n1), near[1 - odd[0]])
    x[0] = first[...] + d[...]


def call(kernel, outs, *args, specs=None, scratch=(), limit=16, products=1):
    return pl.pallas_call(
        kernel,
        out_shape=[jax.ShapeDtypeStruct(shape, dtype) for shape, dtype in outs],
        in_specs=specs or [SMEM if a.ndim == 1 else VMEM for a in args],
        out_specs=[VMEM] * len(outs),
        scratch_shapes=list(scratch),
        compiler_params=pltpu.CompilerParams(vmem_limit_bytes=limit * 1024 * 1024),
        cost_estimate=pl.CostEstimate(flops=products * COST, bytes_accessed=2**20, transcendentals=0),
    )(*args)


def local(right_side, diag_blocks, lower_blocks, upper_blocks, approx_inverse):
    count = lax.axis_size(AXIS)
    near_groups = [[i, i + 1] for i in range(0, count, 2)]
    near_pairs = [(i, i ^ 1) for i in range(count)]
    far_pairs = [(i, ((i + 1) ^ 1) - 1) for i in range(count)]
    far_pairs = [(i, j % count) for i, j in far_pairs]

    def near(v):
        return lax.all_gather(v, AXIS, axis_index_groups=near_groups)

    def swap_near(v):
        return lax.ppermute(v, AXIS, near_pairs)

    def far(v):
        return lax.ppermute(v, AXIS, far_pairs)

    odd = (lax.axis_index(AXIS) % 2).astype(jnp.int32).reshape(1)
    b, lower, upper, diag, inverse = (a[0] for a in (right_side, lower_blocks, upper_blocks, diag_blocks, approx_inverse))
    size, cols = b.shape
    cuts = size // ROWS
    vec = ((size, cols), F32)
    two = ((2, size, cols), F32)
    half = [((size, size), BF16)] * 2
    square = pltpu.VMEM((size, size), F32)
    dma = pltpu.SemaphoreType.DMA

    w, *mats = call(
        first_kernel, [vec] + half * 2, odd, *(pltpu.with_memory_space_constraint(a, pltpu.HBM) for a in (b, lower, upper, inverse)), specs=[SMEM] + [HBM] * 4,
        scratch=[pltpu.VMEM((size, cols), F32), square, square, dma(()), dma((cuts,)), dma((cuts,))], limit=16,
    )
    E, N = mats[:2], mats[2:]
    (sent,) = call(first_pair_kernel, [two], odd, w, near(w), *N, *E)
    got = far(sent)
    h, *mats = call(
        far_block_kernel, [((size // cols, size, cols), F32)] + half * 2, odd, sent, lower, upper, *E,
        specs=[SMEM, ANY] + [VMEM] * 4, products=5,
    )
    F, H = mats[:2], mats[2:]
    k_in = far(h)
    mats = call(near_block_kernel, half * 2, h, diag, *E, *N, specs=[ANY] + [VMEM] * 5, products=5)
    D, J = mats[:2], mats[2:]

    (s,) = call(second_kernel, [vec], sent, got, *H)
    (m,) = call(part_kernel, [vec], odd, near(s), *J)
    f, s_far, *K = call(k_kernel, [vec, vec] + half, sent, got, k_in, *H)
    (parts,) = call(parts_kernel, [two], odd, m, near(f), *J)
    d1, rest = call(step_kernel, [vec, vec], s, s_far, parts, far(parts), b, *H, *K, *D, *F)

    r, w = call(residual_kernel, [vec, vec], odd, near(d1), rest, *N, *E)
    (sent,) = call(pair_kernel, [two], odd, w, near(w), *J)
    pair, s_far = call(seconds_kernel, [two, vec], sent, far(sent), *H, *K)
    (parts,) = call(both_parts_kernel, [two], swap_near(pair), *J)
    d2, rest = call(pair_step_kernel, [vec, vec], pair, s_far, parts, far(parts), r, *H, *K, *D, *F)
    one = ((1, size, cols), F32)
    return tuple(call(last_kernel, [one, one], odd, near(d2), rest, *N, d1, d2))


def solution(mesh):
    spec = P(AXIS, None, None)
    return jax.shard_map(local, mesh=mesh, in_specs=(spec,) * 5, out_specs=(spec, spec), check_vma=False)
```

```python
import jax
import jax.numpy as jnp
from jax import lax
from jax.experimental import pallas as pl
from jax.experimental.pallas import tpu as pltpu
from jax.sharding import PartitionSpec as P

F32 = jnp.float32
BF16 = jnp.bfloat16
VMEM = pl.BlockSpec(memory_space=pltpu.VMEM)
SMEM = pl.BlockSpec(memory_space=pltpu.SMEM)
HBM = pl.BlockSpec(memory_space=pltpu.HBM)
ANY = pl.BlockSpec(memory_space=pl.ANY)
AXIS = "station"
ROWS = 128
COST = 8 * 512 * 512 * 128


def split(v):
    high = v.astype(BF16)
    return high, (v - high.astype(F32)).astype(BF16)


def stack(v):
    return jnp.concatenate(split(v), axis=1)


def rows_times(matrix, rows, both):
    out = jnp.dot(matrix[0][rows, :], both, preferred_element_type=F32)
    out += jnp.dot(matrix[1][rows, :], both, preferred_element_type=F32)
    n = both.shape[1] // 2
    return out[:, :n] + out[:, n:]


def blocks_of(size):
    return [pl.ds(k, ROWS) for k in range(0, size, ROWS)]


def times(matrix, v):
    both = stack(v)
    return jnp.concatenate([rows_times(matrix, rows, both) for rows in blocks_of(v.shape[0])], axis=0)


def put_split(pair, value, *at):
    index = at if at else (...,)
    pair[0][index], pair[1][index] = split(value)


def fetch(source, into, sems):
    copies = []
    for k, rows in enumerate(blocks_of(into.shape[0])):
        copy = pltpu.make_async_copy(source.at[rows], into.at[rows], sems.at[k])
        copy.start()
        copies.append(copy)
    return copies


def fetch_either(is_odd, odd_source, even_source, into, sems):
    copies = []
    for k, rows in enumerate(blocks_of(into.shape[0])):
        copy = pltpu.make_async_copy(odd_source.at[rows], into.at[rows], sems.at[k])
        other = pltpu.make_async_copy(even_source.at[rows], into.at[rows], sems.at[k])
        pl.when(is_odd)(copy.start)
        pl.when(jnp.logical_not(is_odd))(other.start)
        copies.append(copy)
    return copies


def first_kernel(rhs, inverse, w, e0, e1, b_in, e_in, b_sem, e_sem):
    b_copies = fetch(rhs, b_in, b_sem)
    e_copies = fetch(inverse, e_in, e_sem)
    for copy in b_copies:
        copy.wait()
    both = stack(b_in[...])
    for copy, rows in zip(e_copies, blocks_of(inverse.shape[0])):
        copy.wait()
        put_split((e0, e1), e_in[rows], rows)
        w[rows] = rows_times((e0, e1), rows, both)


def blocks_kernel(odd, _, lower, upper, diag, e0, e1, h, h0, h1, j0, j1, n0, n1, f0, f1, d0, d1, n_in, f_in, d_in, n_sem, f_sem, d_sem):
    is_odd = odd[0] == 1
    n_copies = fetch_either(is_odd, lower, upper, n_in, n_sem)
    f_copies = fetch_either(is_odd, upper, lower, f_in, f_sem)
    d_copies = fetch(diag, d_in, d_sem)
    cuts = blocks_of(diag.shape[0])
    cols = h.shape[2]

    def product(parts, to, whole=None):
        for k in range(h.shape[0]):
            at = pl.ds(k * cols, cols)
            both = jnp.concatenate([parts[0][:, at], parts[1][:, at]], axis=1)
            for rows in cuts:
                value = rows_times((e0, e1), rows, both)
                put_split(to, value, rows, at)
                if whole is not None:
                    whole[k, rows] = value

    for copies, source, to in ((n_copies, n_in, (n0, n1)), (f_copies, f_in, (f0, f1)), (d_copies, d_in, (d0, d1))):
        for copy, rows in zip(copies, cuts):
            copy.wait()
            put_split(to, source[rows], rows)
    product((n0, n1), (j0, j1))
    product((f0, f1), (h0, h1), h)


def near_part_kernel(odd, w, near, j0, j1, out):
    out[...] = w[...] - times((j0, j1), near[1 - odd[0]])


def second_kernel(part, got, h0, h1, s):
    s[...] = part[...] - times((h0, h1), got[...])


def part_kernel(odd, near, j0, j1, h, out, h_out):
    out[...] = times((j0, j1), near[1 - odd[0]])


def product_kernel(v, h0, h1, out):
    out[...] = times((h0, h1), v[...])


def parts_kernel(odd, m, near, j0, j1, out):
    out[0] = m[...]
    out[1] = times((j0, j1), near[1 - odd[0]])


def pair_kernel(odd, w, near, j0, j1, out):
    out[0] = w[...]
    out[1] = w[...] - times((j0, j1), near[1 - odd[0]])


def split_kernel(k_in, k0, k1):
    cols = k_in.shape[2]
    for i in range(k_in.shape[0]):
        put_split((k0, k1), k_in[i], slice(None), pl.ds(i * cols, cols))


def sent_kernel(sent, k0, k1, out):
    out[...] = times((k0, k1), sent[0])


def seconds_kernel(sent, got, effect, h0, h1, pair, s_far):
    value = got[1] - effect[...]
    s_far[...] = value
    pair[0] = sent[1] - times((h0, h1), got[0])
    pair[1] = times((h0, h1), value)


def both_parts_kernel(near, j0, j1, out):
    out[0] = times((j0, j1), near[0])
    out[1] = times((j0, j1), near[1])


def step_kernel(s, s_far, effect, sent, got, r, h0, h1, d0, d1, f0, f1, d, rest):
    change = s[...] + sent[1] + times((h0, h1), got[0])
    far = s_far[...] + got[1] + effect[...]
    d[...] = change
    rest[...] = r[...] - times((d0, d1), change) - times((f0, f1), far)


def pair_step_kernel(pair, s_far, effect, sent, got, r, h0, h1, d0, d1, f0, f1, d, rest):
    step_kernel(pair.at[0], s_far, effect, sent, got, r, h0, h1, d0, d1, f0, f1, d, rest)


def residual_kernel(odd, near, rest, n0, n1, e0, e1, r, w):
    value = rest[...] - times((n0, n1), near[1 - odd[0]])
    r[...] = value
    w[...] = times((e0, e1), value)


def last_kernel(odd, near, rest, n0, n1, first, d, x, r):
    r[0] = rest[...] - times((n0, n1), near[1 - odd[0]])
    x[0] = first[...] + d[...]


def call(kernel, outs, *args, specs=None, scratch=(), limit=16, products=1, aliases={}, outs_at=None):
    return pl.pallas_call(
        kernel,
        out_shape=[jax.ShapeDtypeStruct(shape, dtype) for shape, dtype in outs],
        in_specs=specs or [SMEM if a.ndim == 1 else VMEM for a in args],
        out_specs=outs_at or [VMEM] * len(outs),
        input_output_aliases=aliases,
        scratch_shapes=list(scratch),
        compiler_params=pltpu.CompilerParams(vmem_limit_bytes=limit * 1024 * 1024),
        cost_estimate=pl.CostEstimate(flops=products * COST, bytes_accessed=2**20, transcendentals=0),
    )(*args)


def local(right_side, diag_blocks, lower_blocks, upper_blocks, approx_inverse):
    count = lax.axis_size(AXIS)
    near_groups = [[i, i + 1] for i in range(0, count, 2)]
    near_pairs = [(i, i ^ 1) for i in range(count)]
    far_pairs = [(i, ((i + 1) ^ 1) - 1) for i in range(count)]
    far_pairs = [(i, j % count) for i, j in far_pairs]

    def near(v):
        return lax.all_gather(v, AXIS, axis_index_groups=near_groups)

    def swap_near(v):
        return lax.ppermute(v, AXIS, near_pairs)

    def far(v):
        return lax.ppermute(v, AXIS, far_pairs)

    odd = (lax.axis_index(AXIS) % 2).astype(jnp.int32).reshape(1)
    b, lower, upper, diag, inverse = (a[0] for a in (right_side, lower_blocks, upper_blocks, diag_blocks, approx_inverse))
    size, cols = b.shape
    cuts = size // ROWS
    vec = ((size, cols), F32)
    two = ((2, size, cols), F32)
    half = [((size, size), BF16)] * 2
    square = pltpu.VMEM((size, size), F32)
    dmas = pltpu.SemaphoreType.DMA((cuts,))
    blocks = ((size // cols, size, cols), F32)

    def in_hbm(*arrays):
        return [pltpu.with_memory_space_constraint(a, pltpu.HBM) for a in arrays]

    w, *E = call(
        first_kernel, [vec] + half, *in_hbm(b, inverse), specs=[HBM] * 2,
        scratch=[pltpu.VMEM((size, cols), F32), square, dmas, dmas],
    )
    w_far = far(w)
    h, *mats = call(
        blocks_kernel, [blocks] + half * 5, odd, w, *in_hbm(lower, upper, diag), *E,
        specs=[SMEM, ANY] + [HBM] * 3 + [VMEM] * 2, scratch=[square] * 3 + [dmas] * 3, products=10,
    )
    H, J, N, F, D = (mats[i:i + 2] for i in range(0, 10, 2))
    (part,) = call(near_part_kernel, [vec], odd, w, near(w), *J)
    (s,) = call(second_kernel, [vec], part, w_far, *H)
    s_far = far(s)
    m, h = call(
        part_kernel, [vec, blocks], odd, near(s), *J, h,
        specs=[SMEM] + [VMEM] * 3 + [ANY], outs_at=[VMEM, ANY], aliases={4: 1},
    )
    k_in = far(h)
    (f,) = call(product_kernel, [vec], s_far, *H, products=20)
    (parts,) = call(parts_kernel, [two], odd, m, near(f), *J)
    got = far(parts)
    K = call(split_kernel, half, k_in)
    (effect,) = call(sent_kernel, [vec], parts, *K)
    d1, rest = call(step_kernel, [vec, vec], s, s_far, effect, parts, got, b, *H, *D, *F)

    r, w = call(residual_kernel, [vec, vec], odd, near(d1), rest, *N, *E)
    (sent,) = call(pair_kernel, [two], odd, w, near(w), *J)
    got = far(sent)
    (effect,) = call(sent_kernel, [vec], sent, *K)
    pair, s_far = call(seconds_kernel, [two, vec], sent, got, effect, *H)
    (parts,) = call(both_parts_kernel, [two], swap_near(pair), *J)
    got = far(parts)
    (effect,) = call(sent_kernel, [vec], parts, *K)
    d2, rest = call(pair_step_kernel, [vec, vec], pair, s_far, effect, parts, got, r, *H, *D, *F)
    one = ((1, size, cols), F32)
    return tuple(call(last_kernel, [one, one], odd, near(d2), rest, *N, d1, d2))


def solution(mesh):
    spec = P(AXIS, None, None)
    return jax.shard_map(local, mesh=mesh, in_specs=(spec,) * 5, out_specs=(spec, spec), check_vma=False)
```

```python
import jax
import jax.numpy as jnp
from jax import lax
from jax.experimental import pallas as pl
from jax.experimental.pallas import tpu as pltpu
from jax.sharding import PartitionSpec as P

F32 = jnp.float32
BF16 = jnp.bfloat16
VMEM = pl.BlockSpec(memory_space=pltpu.VMEM)
SMEM = pl.BlockSpec(memory_space=pltpu.SMEM)
HBM = pl.BlockSpec(memory_space=pltpu.HBM)
ANY = pl.BlockSpec(memory_space=pl.ANY)
AXIS = "station"
ROWS = 128
COST = 8 * 512 * 512 * 128


def split(v):
    high = v.astype(BF16)
    return high, (v - high.astype(F32)).astype(BF16)


def stack(v):
    return jnp.concatenate(split(v), axis=1)


def rows_times(matrix, rows, both):
    out = jnp.dot(matrix[0][rows, :], both, preferred_element_type=F32)
    out += jnp.dot(matrix[1][rows, :], both, preferred_element_type=F32)
    n = both.shape[1] // 2
    return out[:, :n] + out[:, n:]


def blocks_of(size):
    return [pl.ds(k, ROWS) for k in range(0, size, ROWS)]


def times(matrix, v):
    both = stack(v)
    return jnp.concatenate([rows_times(matrix, rows, both) for rows in blocks_of(v.shape[0])], axis=0)


def put_split(pair, value, *at):
    index = at if at else (...,)
    pair[0][index], pair[1][index] = split(value)


def fetch(source, into, sems):
    copies = []
    for k, rows in enumerate(blocks_of(into.shape[0])):
        copy = pltpu.make_async_copy(source.at[rows], into.at[rows], sems.at[k])
        copy.start()
        copies.append(copy)
    return copies


def fetch_either(is_odd, odd_source, even_source, into, sems):
    copies = []
    for k, rows in enumerate(blocks_of(into.shape[0])):
        copy = pltpu.make_async_copy(odd_source.at[rows], into.at[rows], sems.at[k])
        other = pltpu.make_async_copy(even_source.at[rows], into.at[rows], sems.at[k])
        pl.when(is_odd)(copy.start)
        pl.when(jnp.logical_not(is_odd))(other.start)
        copies.append(copy)
    return copies


def first_kernel(rhs, inverse, w, e0, e1, b_in, e_in, b_sem, e_sem):
    b_copies = fetch(rhs, b_in, b_sem)
    e_copies = fetch(inverse, e_in, e_sem)
    for copy in b_copies:
        copy.wait()
    both = stack(b_in[...])
    for copy, rows in zip(e_copies, blocks_of(inverse.shape[0])):
        copy.wait()
        put_split((e0, e1), e_in[rows], rows)
        w[rows] = rows_times((e0, e1), rows, both)


def blocks_kernel(odd, _, lower, upper, diag, e0, e1, h, h0, h1, j0, j1, n0, n1, f0, f1, d0, d1, n_in, f_in, d_in, n_sem, f_sem, d_sem):
    is_odd = odd[0] == 1
    n_copies = fetch_either(is_odd, lower, upper, n_in, n_sem)
    f_copies = fetch_either(is_odd, upper, lower, f_in, f_sem)
    d_copies = fetch(diag, d_in, d_sem)
    cuts = blocks_of(diag.shape[0])
    cols = h.shape[2]

    def product(parts, to, whole=None):
        for k in range(h.shape[0]):
            at = pl.ds(k * cols, cols)
            both = jnp.concatenate([parts[0][:, at], parts[1][:, at]], axis=1)
            for rows in cuts:
                value = rows_times((e0, e1), rows, both)
                put_split(to, value, rows, at)
                if whole is not None:
                    whole[k, rows] = value

    for copies, source, to in ((n_copies, n_in, (n0, n1)), (f_copies, f_in, (f0, f1)), (d_copies, d_in, (d0, d1))):
        for copy, rows in zip(copies, cuts):
            copy.wait()
            put_split(to, source[rows], rows)
    product((n0, n1), (j0, j1))
    product((f0, f1), (h0, h1), h)


def near_part_kernel(odd, w, near, j0, j1, out):
    out[...] = w[...] - times((j0, j1), near[1 - odd[0]])


def second_kernel(part, got, h0, h1, s):
    s[...] = part[...] - times((h0, h1), got[...])


def part_kernel(odd, s, near, j0, j1, out):
    out[0] = s[...]
    out[1] = times((j0, j1), near[1 - odd[0]])


def part_and_block_kernel(odd, s, near, j0, j1, h, out, h_out):
    part_kernel(odd, s, near, j0, j1, out)


def front_kernel(sent, got, h0, h1, f, g):
    n = f.shape[1]
    both = times((h0, h1), jnp.concatenate([got[0], got[1]], axis=1))
    f[...] = both[:, :n]
    g[...] = sent[0] + both[:, n:]


def step_kernel(odd, g, near, j0, j1, d):
    d[...] = g[...] + times((j0, j1), near[1 - odd[0]])


def step_rest_kernel(odd, g, near, r, j0, j1, d0, d1, d, rest):
    step_kernel(odd, g, near, j0, j1, d)
    rest[...] = r[...] - times((d0, d1), d[...])


def again_kernel(odd, near, rest, d, n0, n1, e0, e1, out, rest_out):
    value = rest[...] - times((n0, n1), near[1 - odd[0]])
    rest_out[...] = value
    out[0] = d[...]
    out[1] = times((e0, e1), value)


def split_kernel(k_in, k0, k1):
    cols = k_in.shape[2]
    for i in range(k_in.shape[0]):
        put_split((k0, k1), k_in[i], slice(None), pl.ds(i * cols, cols))


def sent_kernel(sent, k0, k1, out):
    out[...] = times((k0, k1), sent[0])


def both_w_kernel(sent, got, effect, h0, h1, w, base):
    n = w.shape[1]
    both = times((h0, h1), jnp.concatenate([got[0], got[1] - effect[...]], axis=1))
    value = sent[1] - both[:, :n]
    w[...] = value
    base[...] = value - both[:, n:]


def base_kernel(odd, base, near, j0, j1, s):
    s[...] = base[...] - times((j0, j1), near[1 - odd[0]])


def residual_kernel(_, rest, got, f0, f1, r):
    r[...] = rest[...] - times((f0, f1), got[0])


def sum_kernel(odd, near, r, d, first, n0, n1, d0, d1, rest, x):
    rest[...] = r[...] - times((d0, d1), d[...]) - times((n0, n1), near[1 - odd[0]])
    x[0] = first[...] + d[...]


def last_kernel(rest, got, f0, f1, r):
    r[0] = rest[...] - times((f0, f1), got[...])


def call(kernel, outs, *args, specs=None, scratch=(), limit=16, products=1, aliases={}, outs_at=None):
    return pl.pallas_call(
        kernel,
        out_shape=[jax.ShapeDtypeStruct(shape, dtype) for shape, dtype in outs],
        in_specs=specs or [SMEM if a.ndim == 1 else VMEM for a in args],
        out_specs=outs_at or [VMEM] * len(outs),
        input_output_aliases=aliases,
        scratch_shapes=list(scratch),
        compiler_params=pltpu.CompilerParams(vmem_limit_bytes=limit * 1024 * 1024),
        cost_estimate=pl.CostEstimate(flops=products * COST, bytes_accessed=2**20, transcendentals=0),
    )(*args)


def local(right_side, diag_blocks, lower_blocks, upper_blocks, approx_inverse):
    count = lax.axis_size(AXIS)
    near_groups = [[i, i + 1] for i in range(0, count, 2)]
    near_pairs = [(i, i ^ 1) for i in range(count)]
    far_pairs = [(i, ((i + 1) ^ 1) - 1) for i in range(count)]
    far_pairs = [(i, j % count) for i, j in far_pairs]

    def near(v):
        return lax.all_gather(v, AXIS, axis_index_groups=near_groups)

    def swap_near(v):
        return lax.ppermute(v, AXIS, near_pairs)

    def far(v):
        return lax.ppermute(v, AXIS, far_pairs)

    odd = (lax.axis_index(AXIS) % 2).astype(jnp.int32).reshape(1)
    b, lower, upper, diag, inverse = (a[0] for a in (right_side, lower_blocks, upper_blocks, diag_blocks, approx_inverse))
    size, cols = b.shape
    cuts = size // ROWS
    vec = ((size, cols), F32)
    two = ((2, size, cols), F32)
    half = [((size, size), BF16)] * 2
    square = pltpu.VMEM((size, size), F32)
    dmas = pltpu.SemaphoreType.DMA((cuts,))
    blocks = ((size // cols, size, cols), F32)

    def in_hbm(*arrays):
        return [pltpu.with_memory_space_constraint(a, pltpu.HBM) for a in arrays]

    w, *E = call(
        first_kernel, [vec] + half, *in_hbm(b, inverse), specs=[HBM] * 2,
        scratch=[pltpu.VMEM((size, cols), F32), square, dmas, dmas],
    )
    w_far = far(w)
    h, *mats = call(
        blocks_kernel, [blocks] + half * 5, odd, w, *in_hbm(lower, upper, diag), *E,
        specs=[SMEM, ANY] + [HBM] * 3 + [VMEM] * 2, scratch=[square] * 3 + [dmas] * 3, products=10,
    )
    H, J, N, F, D = (mats[i:i + 2] for i in range(0, 10, 2))
    (part,) = call(near_part_kernel, [vec], odd, w, near(w), *J)
    (s,) = call(second_kernel, [vec], part, w_far, *H)
    sent, h = call(
        part_and_block_kernel, [two, blocks], odd, s, near(s), *J, h,
        specs=[SMEM] + [VMEM] * 4 + [ANY], outs_at=[VMEM, ANY], aliases={5: 1},
    )
    got = far(sent)
    k_in = far(h)
    f, g = call(front_kernel, [vec, vec], sent, got, *H, products=20)
    first, rest = call(step_rest_kernel, [vec, vec], odd, g, near(f), b, *J, *D)
    sent, rest = call(again_kernel, [two, vec], odd, near(first), rest, first, *N, *E)
    got = far(sent)
    K = call(split_kernel, half, k_in)
    (effect,) = call(sent_kernel, [vec], sent, *K)
    w, base = call(both_w_kernel, [vec, vec], sent, got, effect, *H)

    (s,) = call(base_kernel, [vec], odd, base, near(w), *J)
    (sent,) = call(part_kernel, [two], odd, s, near(s), *J)
    (r,) = call(residual_kernel, [vec], sent, rest, got, *F, specs=[ANY] + [VMEM] * 4)
    f, g = call(front_kernel, [vec, vec], sent, far(sent), *H)
    (d,) = call(step_kernel, [vec], odd, g, near(f), *J)
    got = far(d)
    one = ((1, size, cols), F32)
    rest, x = call(sum_kernel, [vec, one], odd, near(d), r, d, first, *N, *D)
    (r,) = call(last_kernel, [one], rest, got, *F)
    return x, r


def solution(mesh):
    spec = P(AXIS, None, None)
    return jax.shard_map(local, mesh=mesh, in_specs=(spec,) * 5, out_specs=(spec, spec), check_vma=False)
```

```python
import jax
import jax.numpy as jnp
from jax import lax
from jax.experimental import pallas as pl
from jax.experimental.pallas import tpu as pltpu
from jax.sharding import PartitionSpec as P

F32 = jnp.float32
BF16 = jnp.bfloat16
VMEM = pl.BlockSpec(memory_space=pltpu.VMEM)
SMEM = pl.BlockSpec(memory_space=pltpu.SMEM)
HBM = pl.BlockSpec(memory_space=pltpu.HBM)
ANY = pl.BlockSpec(memory_space=pl.ANY)
AXIS = "station"
ROWS = 128
COST = 8 * 512 * 512 * 128


def split(v):
    high = v.astype(BF16)
    return high, (v - high.astype(F32)).astype(BF16)


def stack(v):
    return jnp.concatenate(split(v), axis=1)


def rows_times(matrix, rows, both):
    out = jnp.dot(matrix[0][rows, :], both, preferred_element_type=F32)
    out += jnp.dot(matrix[1][rows, :], both, preferred_element_type=F32)
    n = both.shape[1] // 2
    return out[:, :n] + out[:, n:]


def blocks_of(size):
    return [pl.ds(k, ROWS) for k in range(0, size, ROWS)]


def times(matrix, v):
    both = stack(v)
    return jnp.concatenate([rows_times(matrix, rows, both) for rows in blocks_of(v.shape[0])], axis=0)


def put_split(pair, value, *at):
    index = at if at else (...,)
    pair[0][index], pair[1][index] = split(value)


def fetch(source, into, sems):
    copies = []
    for k, rows in enumerate(blocks_of(into.shape[0])):
        copy = pltpu.make_async_copy(source.at[rows], into.at[rows], sems.at[k])
        copy.start()
        copies.append(copy)
    return copies


def fetch_either(is_odd, odd_source, even_source, into, sems):
    copies = []
    for k, rows in enumerate(blocks_of(into.shape[0])):
        copy = pltpu.make_async_copy(odd_source.at[rows], into.at[rows], sems.at[k])
        other = pltpu.make_async_copy(even_source.at[rows], into.at[rows], sems.at[k])
        pl.when(is_odd)(copy.start)
        pl.when(jnp.logical_not(is_odd))(other.start)
        copies.append(copy)
    return copies


def first_kernel(rhs, inverse, w, b_in, e0, e1, e_in, b_sem, e_sem):
    b_copy = pltpu.make_async_copy(rhs, b_in, b_sem)
    e_copy = pltpu.make_async_copy(inverse, e_in, e_sem)
    b_copy.start()
    e_copy.start()
    b_copy.wait()
    both = stack(b_in[...])
    e_copy.wait()
    put_split((e0, e1), e_in[...])
    for rows in blocks_of(inverse.shape[0]):
        w[rows] = rows_times((e0, e1), rows, both)


def blocks_kernel(odd, _, lower, upper, diag, e0, e1, h, j, h0, h1, j0, j1, n0, n1, f0, f1, d0, d1, n_in, f_in, d_in, n_sem, f_sem, d_sem):
    is_odd = odd[0] == 1
    n_copies = fetch_either(is_odd, lower, upper, n_in, n_sem)
    f_copies = fetch_either(is_odd, upper, lower, f_in, f_sem)
    d_copies = fetch(diag, d_in, d_sem)
    cuts = blocks_of(diag.shape[0])
    cols = h.shape[2]

    def product(parts, to, whole):
        for k in range(0, h.shape[0], 2):
            at = pl.ds(k * cols, 2 * cols)
            both = jnp.concatenate([parts[0][:, at], parts[1][:, at]], axis=1)
            for rows in cuts:
                value = rows_times((e0, e1), rows, both)
                put_split(to, value, rows, at)
                whole[k, rows] = value[:, :cols]
                whole[k + 1, rows] = value[:, cols:]

    for copies, source, to in ((n_copies, n_in, (n0, n1)), (f_copies, f_in, (f0, f1)), (d_copies, d_in, (d0, d1))):
        for copy, rows in zip(copies, cuts):
            copy.wait()
            put_split(to, source[rows], rows)
    product((n0, n1), (j0, j1), j)
    product((f0, f1), (h0, h1), h)


def near_part_kernel(odd, w, near, j0, j1, out):
    out[...] = w[...] - times((j0, j1), near[1 - odd[0]])


def second_kernel(part, got, h0, h1, s):
    s[...] = part[...] - times((h0, h1), got[...])


def part_kernel(odd, s, near, j0, j1, out):
    out[0] = s[...]
    out[1] = times((j0, j1), near[1 - odd[0]])


def part_and_blocks_kernel(odd, s, near, j0, j1, h, j, out, h_out, j_out):
    part_kernel(odd, s, near, j0, j1, out)


def twice_kernel(near_j, j0, j1, q0, q1):
    cols = near_j.shape[2]
    for k in range(0, near_j.shape[0], 2):
        both = stack(jnp.concatenate([near_j[k], near_j[k + 1]], axis=1))
        for rows in blocks_of(q0.shape[0]):
            put_split((q0, q1), rows_times((j0, j1), rows, both), rows, pl.ds(k * cols, 2 * cols))


def two_times(matrix, pair):
    n = pair.shape[2]
    both = times(matrix, jnp.concatenate([pair[0], pair[1]], axis=1))
    return both[:, :n], both[:, n:]


def front_kernel(sent, got, h0, h1, pair):
    f, change = two_times((h0, h1), got)
    pair[0] = f
    pair[1] = sent[0] + change


def last_front_kernel(_, sent, got, h0, h1, f, g):
    value, change = two_times((h0, h1), got)
    f[...] = value
    g[...] = sent[0] + change


def sent_kernel(sent, k0, k1, out):
    out[...] = times((k0, k1), sent[0])


def again_kernel(pair, near, effect, r, j0, j1, d0, d1, e0, e1, out, rest):
    own, other = two_times((j0, j1), near)
    change = pair[1] + own
    value = r[...] - times((d0, d1), change)
    rest[...] = value
    out[0] = change
    out[1] = times((e0, e1), value) - other - effect[...]


def near_rest_kernel(odd, near, before, n0, n1, rest):
    rest[...] = before[...] - times((n0, n1), near[1 - odd[0]])


def split_kernel(k_in, k0, k1):
    cols = k_in.shape[2]
    for i in range(k_in.shape[0]):
        put_split((k0, k1), k_in[i], slice(None), pl.ds(i * cols, cols))


def both_w_kernel(sent, got, effect, h0, h1, pair):
    n = pair.shape[2]
    both = times((h0, h1), jnp.concatenate([got[0], got[1] - effect[...]], axis=1))
    w = sent[1] - both[:, :n]
    pair[0] = w
    pair[1] = w - both[:, n:]


def both_s_kernel(pair, near, effect, j0, j1, out):
    own, other = two_times((j0, j1), near)
    out[0] = pair[1] - own
    out[1] = other - effect[...]


def step_kernel(odd, g, near, j0, j1, d):
    d[...] = g[...] + times((j0, j1), near[1 - odd[0]])


def residual_kernel(_, rest, got, f0, f1, r):
    r[...] = rest[...] - times((f0, f1), got[0])


def sum_kernel(r, d, first, d0, d1, rest, x):
    rest[...] = r[...] - times((d0, d1), d[...])
    x[0] = first[0] + d[...]


def swapped_rest_kernel(near, before, n0, n1, rest):
    rest[...] = before[...] - times((n0, n1), near[...])


def last_kernel(rest, got, f0, f1, r):
    r[0] = rest[...] - times((f0, f1), got[...])


def call(kernel, outs, *args, specs=None, scratch=(), limit=16, products=1, aliases={}, outs_at=None):
    return pl.pallas_call(
        kernel,
        out_shape=[jax.ShapeDtypeStruct(shape, dtype) for shape, dtype in outs],
        in_specs=specs or [SMEM if a.ndim == 1 else VMEM for a in args],
        out_specs=outs_at or [VMEM] * len(outs),
        input_output_aliases=aliases,
        scratch_shapes=list(scratch),
        compiler_params=pltpu.CompilerParams(vmem_limit_bytes=limit * 1024 * 1024),
        cost_estimate=pl.CostEstimate(flops=products * COST, bytes_accessed=2**20, transcendentals=0),
    )(*args)


def local(right_side, diag_blocks, lower_blocks, upper_blocks, approx_inverse):
    count = lax.axis_size(AXIS)
    near_groups = [[i, i + 1] for i in range(0, count, 2)]
    near_pairs = [(i, i ^ 1) for i in range(count)]
    far_pairs = [(i, ((i + 1) ^ 1) - 1) for i in range(count)]
    far_pairs = [(i, j % count) for i, j in far_pairs]

    def near(v):
        return lax.all_gather(v, AXIS, axis_index_groups=near_groups)

    def swap_near(v):
        return lax.ppermute(v, AXIS, near_pairs)

    def far(v):
        return lax.ppermute(v, AXIS, far_pairs)

    odd = (lax.axis_index(AXIS) % 2).astype(jnp.int32).reshape(1)
    b, lower, upper, diag, inverse = (a[0] for a in (right_side, lower_blocks, upper_blocks, diag_blocks, approx_inverse))
    size, cols = b.shape
    cuts = size // ROWS
    vec = ((size, cols), F32)
    two = ((2, size, cols), F32)
    half = [((size, size), BF16)] * 2
    square = pltpu.VMEM((size, size), F32)
    dmas = pltpu.SemaphoreType.DMA((cuts,))
    blocks = ((size // cols, size, cols), F32)

    def in_hbm(*arrays):
        return [pltpu.with_memory_space_constraint(a, pltpu.HBM) for a in arrays]

    w, b, *E = call(
        first_kernel, [vec, vec] + half, *in_hbm(b, inverse), specs=[HBM] * 2,
        scratch=[square] + [pltpu.SemaphoreType.DMA(())] * 2,
    )
    w_far = far(w)
    h, j, *mats = call(
        blocks_kernel, [blocks] * 2 + half * 5, odd, w, *in_hbm(lower, upper, diag), *E,
        specs=[SMEM, ANY] + [HBM] * 3 + [VMEM] * 2, scratch=[square] * 3 + [dmas] * 3, products=10,
    )
    H, J, N, F, D = (mats[i:i + 2] for i in range(0, 10, 2))
    (part,) = call(near_part_kernel, [vec], odd, w, near(w), *J)
    (s,) = call(second_kernel, [vec], part, w_far, *H)
    sent, h, j = call(
        part_and_blocks_kernel, [two, blocks, blocks], odd, s, near(s), *J, h, j,
        specs=[SMEM] + [VMEM] * 4 + [ANY] * 2, outs_at=[VMEM, ANY, ANY], aliases={5: 1, 6: 2},
    )
    got = far(sent)
    k_in = far(h)
    Q = call(twice_kernel, half, swap_near(j), *J)
    (pair,) = call(front_kernel, [two], sent, got, *H, products=20)
    other = swap_near(pair)
    (effect,) = call(sent_kernel, [vec], pair, *Q, products=1)
    sent, rest = call(again_kernel, [two, vec], pair, other, effect, b, *J, *D, *E)
    got = far(sent)
    K = call(split_kernel, half, k_in)
    (effect,) = call(sent_kernel, [vec], sent, *K)
    (rest,) = call(near_rest_kernel, [vec], odd, near(sent[0]), rest, *N)
    first = sent
    (pair,) = call(both_w_kernel, [two], sent, got, effect, *H)

    other = swap_near(pair)
    (effect,) = call(sent_kernel, [vec], pair, *Q)
    (sent,) = call(both_s_kernel, [two], pair, other, effect, *J)
    (r,) = call(residual_kernel, [vec], sent, rest, got, *F, specs=[ANY] + [VMEM] * 4)
    f, g = call(last_front_kernel, [vec, vec], r, sent, far(sent), *H, specs=[ANY] + [VMEM] * 4)
    (d,) = call(step_kernel, [vec], odd, g, near(f), *J)
    got = far(d)
    one = ((1, size, cols), F32)
    other = swap_near(d)
    rest, x = call(sum_kernel, [vec, one], r, d, first, *D, products=20)
    (rest,) = call(swapped_rest_kernel, [vec], other, rest, *N)
    (r,) = call(last_kernel, [one], rest, got, *F)
    return x, r


def solution(mesh):
    spec = P(AXIS, None, None)
    return jax.shard_map(local, mesh=mesh, in_specs=(spec,) * 5, out_specs=(spec, spec), check_vma=False)
```

```python
import jax
import jax.numpy as jnp
from jax import lax
from jax.experimental import pallas as pl
from jax.experimental.pallas import tpu as pltpu
from jax.sharding import PartitionSpec as P

F32 = jnp.float32
BF16 = jnp.bfloat16
VMEM = pl.BlockSpec(memory_space=pltpu.VMEM)
SMEM = pl.BlockSpec(memory_space=pltpu.SMEM)
HBM = pl.BlockSpec(memory_space=pltpu.HBM)
ANY = pl.BlockSpec(memory_space=pl.ANY)
AXIS = "station"
ROWS = 128
COST = 8 * 512 * 512 * 128


def split(v):
    high = v.astype(BF16)
    return high, (v - high.astype(F32)).astype(BF16)


def stack(v):
    return jnp.concatenate(split(v), axis=1)


def rows_times(matrix, rows, both):
    parts = jnp.concatenate([matrix[0][rows, :], matrix[1][rows, :]], axis=0)
    out = jnp.dot(parts, both, preferred_element_type=F32)
    out = out[:ROWS] + out[ROWS:]
    n = both.shape[1] // 2
    return out[:, :n] + out[:, n:]


def blocks_of(size):
    return [pl.ds(k, ROWS) for k in range(0, size, ROWS)]


def times(matrix, v):
    both = stack(v)
    return jnp.concatenate([rows_times(matrix, rows, both) for rows in blocks_of(v.shape[0])], axis=0)


def put_split(pair, value, *at):
    index = at if at else (...,)
    pair[0][index], pair[1][index] = split(value)


def fetch(source, into, sems):
    copies = []
    for k, rows in enumerate(blocks_of(into.shape[0])):
        copy = pltpu.make_async_copy(source.at[rows], into.at[rows], sems.at[k])
        copy.start()
        copies.append(copy)
    return copies


def fetch_either(is_odd, odd_source, even_source, into, sems):
    copies = []
    for k, rows in enumerate(blocks_of(into.shape[0])):
        copy = pltpu.make_async_copy(odd_source.at[rows], into.at[rows], sems.at[k])
        other = pltpu.make_async_copy(even_source.at[rows], into.at[rows], sems.at[k])
        pl.when(is_odd)(copy.start)
        pl.when(jnp.logical_not(is_odd))(other.start)
        copies.append(copy)
    return copies


def first_kernel(rhs, inverse, w, b_in, e0, e1, e_in, b_sem, e_sem):
    b_copy = pltpu.make_async_copy(rhs, b_in, b_sem)
    e_copy = pltpu.make_async_copy(inverse, e_in, e_sem)
    b_copy.start()
    e_copy.start()
    b_copy.wait()
    both = stack(b_in[...])
    e_copy.wait()
    put_split((e0, e1), e_in[...])
    for rows in blocks_of(inverse.shape[0]):
        w[rows] = rows_times((e0, e1), rows, both)


def blocks_kernel(odd, _, lower, upper, diag, e0, e1, h, j, h0, h1, j0, j1, n0, n1, f0, f1, d0, d1, n_in, f_in, d_in, n_sem, f_sem, d_sem):
    is_odd = odd[0] == 1
    n_copies = fetch_either(is_odd, lower, upper, n_in, n_sem)
    f_copies = fetch_either(is_odd, upper, lower, f_in, f_sem)
    d_copies = fetch(diag, d_in, d_sem)
    cuts = blocks_of(diag.shape[0])
    cols = h.shape[2]

    def product(parts, to, whole):
        for k in range(0, h.shape[0], 2):
            at = pl.ds(k * cols, 2 * cols)
            both = jnp.concatenate([parts[0][:, at], parts[1][:, at]], axis=1)
            for rows in cuts:
                value = rows_times((e0, e1), rows, both)
                put_split(to, value, rows, at)
                whole[k, rows] = value[:, :cols]
                whole[k + 1, rows] = value[:, cols:]

    for copies, source, to in ((n_copies, n_in, (n0, n1)), (f_copies, f_in, (f0, f1)), (d_copies, d_in, (d0, d1))):
        for copy, rows in zip(copies, cuts):
            copy.wait()
            put_split(to, source[rows], rows)
    product((n0, n1), (j0, j1), j)
    product((f0, f1), (h0, h1), h)


def near_part_kernel(odd, w, near, j0, j1, out):
    out[...] = w[...] - times((j0, j1), near[1 - odd[0]])


def second_kernel(part, got, h0, h1, s):
    s[...] = part[...] - times((h0, h1), got[...])


def part_kernel(odd, s, near, j0, j1, out):
    out[0] = s[...]
    out[1] = times((j0, j1), near[1 - odd[0]])


def part_and_blocks_kernel(odd, s, near, j0, j1, h, j, out, h_out, j_out):
    part_kernel(odd, s, near, j0, j1, out)


def twice_kernel(near_j, j0, j1, q0, q1):
    cols = near_j.shape[2]
    for k in range(0, near_j.shape[0], 2):
        both = stack(jnp.concatenate([near_j[k], near_j[k + 1]], axis=1))
        for rows in blocks_of(q0.shape[0]):
            put_split((q0, q1), rows_times((j0, j1), rows, both), rows, pl.ds(k * cols, 2 * cols))


def two_times(matrix, pair):
    n = pair.shape[2]
    both = times(matrix, jnp.concatenate([pair[0], pair[1]], axis=1))
    return both[:, :n], both[:, n:]


def front_kernel(sent, got, h0, h1, pair):
    f, change = two_times((h0, h1), got)
    pair[0] = f
    pair[1] = sent[0] + change


def last_front_kernel(_, sent, got, h0, h1, f, g):
    value, change = two_times((h0, h1), got)
    f[...] = value
    g[...] = sent[0] + change


def sent_kernel(sent, k0, k1, out):
    out[...] = times((k0, k1), sent[0])


def again_kernel(pair, near, effect, r, j0, j1, d0, d1, e0, e1, out, rest):
    own, other = two_times((j0, j1), near)
    change = pair[1] + own
    value = r[...] - times((d0, d1), change)
    rest[...] = value
    out[0] = change
    out[1] = times((e0, e1), value) - other - effect[...]


def near_rest_kernel(odd, near, before, n0, n1, rest):
    rest[...] = before[...] - times((n0, n1), near[1 - odd[0]])


def split_kernel(k_in, k0, k1):
    cols = k_in.shape[2]
    for i in range(k_in.shape[0]):
        put_split((k0, k1), k_in[i], slice(None), pl.ds(i * cols, cols))


def both_w_kernel(sent, got, effect, h0, h1, pair):
    n = pair.shape[2]
    both = times((h0, h1), jnp.concatenate([got[0], got[1] - effect[...]], axis=1))
    w = sent[1] - both[:, :n]
    pair[0] = w
    pair[1] = w - both[:, n:]


def both_s_kernel(pair, near, effect, j0, j1, out):
    own, other = two_times((j0, j1), near)
    out[0] = pair[1] - own
    out[1] = other - effect[...]


def step_kernel(odd, g, near, j0, j1, d):
    d[...] = g[...] + times((j0, j1), near[1 - odd[0]])


def residual_kernel(_, rest, got, f0, f1, r):
    r[...] = rest[...] - times((f0, f1), got[0])


def last_kernel(odd, near, r_before, got, first, d, d0, d1, n0, n1, f0, f1, x, r):
    change = d[...]
    x[0] = first[0] + change
    rest = r_before[...] - times((d0, d1), change) - times((f0, f1), got[...])
    r[0] = rest - times((n0, n1), near[1 - odd[0]])


def call(kernel, outs, *args, specs=None, scratch=(), limit=16, products=1, aliases={}, outs_at=None):
    return pl.pallas_call(
        kernel,
        out_shape=[jax.ShapeDtypeStruct(shape, dtype) for shape, dtype in outs],
        in_specs=specs or [SMEM if a.ndim == 1 else VMEM for a in args],
        out_specs=outs_at or [VMEM] * len(outs),
        input_output_aliases=aliases,
        scratch_shapes=list(scratch),
        compiler_params=pltpu.CompilerParams(vmem_limit_bytes=limit * 1024 * 1024),
        cost_estimate=pl.CostEstimate(flops=products * COST, bytes_accessed=2**20, transcendentals=0),
    )(*args)


def local(right_side, diag_blocks, lower_blocks, upper_blocks, approx_inverse):
    count = lax.axis_size(AXIS)
    near_groups = [[i, i + 1] for i in range(0, count, 2)]
    near_pairs = [(i, i ^ 1) for i in range(count)]
    far_pairs = [(i, ((i + 1) ^ 1) - 1) for i in range(count)]
    far_pairs = [(i, j % count) for i, j in far_pairs]

    def near(v):
        return lax.all_gather(v, AXIS, axis_index_groups=near_groups)

    def swap_near(v):
        return lax.ppermute(v, AXIS, near_pairs)

    def far(v):
        return lax.ppermute(v, AXIS, far_pairs)

    odd = (lax.axis_index(AXIS) % 2).astype(jnp.int32).reshape(1)
    b, lower, upper, diag, inverse = (a[0] for a in (right_side, lower_blocks, upper_blocks, diag_blocks, approx_inverse))
    size, cols = b.shape
    cuts = size // ROWS
    vec = ((size, cols), F32)
    two = ((2, size, cols), F32)
    half = [((size, size), BF16)] * 2
    square = pltpu.VMEM((size, size), F32)
    dmas = pltpu.SemaphoreType.DMA((cuts,))
    blocks = ((size // cols, size, cols), F32)

    def in_hbm(*arrays):
        return [pltpu.with_memory_space_constraint(a, pltpu.HBM) for a in arrays]

    w, b, *E = call(
        first_kernel, [vec, vec] + half, *in_hbm(b, inverse), specs=[HBM] * 2,
        scratch=[square] + [pltpu.SemaphoreType.DMA(())] * 2,
    )
    w_far = far(w)
    h, j, *mats = call(
        blocks_kernel, [blocks] * 2 + half * 5, odd, w, *in_hbm(lower, upper, diag), *E,
        specs=[SMEM, ANY] + [HBM] * 3 + [VMEM] * 2, scratch=[square] * 3 + [dmas] * 3, products=10,
    )
    H, J, N, F, D = (mats[i:i + 2] for i in range(0, 10, 2))
    (part,) = call(near_part_kernel, [vec], odd, w, near(w), *J)
    (s,) = call(second_kernel, [vec], part, w_far, *H)
    sent, h, j = call(
        part_and_blocks_kernel, [two, blocks, blocks], odd, s, near(s), *J, h, j,
        specs=[SMEM] + [VMEM] * 4 + [ANY] * 2, outs_at=[VMEM, ANY, ANY], aliases={5: 1, 6: 2},
    )
    got = far(sent)
    k_in = far(h)
    Q = call(twice_kernel, half, swap_near(j), *J)
    (pair,) = call(front_kernel, [two], sent, got, *H, products=20)
    other = swap_near(pair)
    (effect,) = call(sent_kernel, [vec], pair, *Q, products=1)
    sent, rest = call(again_kernel, [two, vec], pair, other, effect, b, *J, *D, *E)
    got = far(sent)
    K = call(split_kernel, half, k_in)
    (effect,) = call(sent_kernel, [vec], sent, *K)
    (rest,) = call(near_rest_kernel, [vec], odd, near(sent[0]), rest, *N)
    first = sent
    (pair,) = call(both_w_kernel, [two], sent, got, effect, *H)

    other = swap_near(pair)
    (effect,) = call(sent_kernel, [vec], pair, *Q)
    (sent,) = call(both_s_kernel, [two], pair, other, effect, *J)
    (r,) = call(residual_kernel, [vec], sent, rest, got, *F, specs=[ANY] + [VMEM] * 4)
    f, g = call(last_front_kernel, [vec, vec], r, sent, far(sent), *H, specs=[ANY] + [VMEM] * 4)
    (d,) = call(step_kernel, [vec], odd, g, near(f), *J)
    got = far(d)
    one = ((1, size, cols), F32)
    return tuple(call(last_kernel, [one, one], odd, near(d), r, got, first, d, *D, *N, *F))


def solution(mesh):
    spec = P(AXIS, None, None)
    return jax.shard_map(local, mesh=mesh, in_specs=(spec,) * 5, out_specs=(spec, spec), check_vma=False)
```
